256 devices in a mesh: ctx: 64 (over z_lo, y, x, core), ch: 4 (over z_hi).
Axes of the slice: x: 4, y: 4, z: 8 (z_hi: 4, z_lo: 2; z = z_hi * 2 + z_lo), core: 2. Of those that a mesh axis runs over, the one named last changes fastest.
Arguments:
- queries: bfloat16 [8192, 16384], P('ch', 'ctx'), may hold values from -6 to 6
- keys: bfloat16 [8192, 16384], P('ch', 'ctx'), may hold values from -6 to 6
- values: bfloat16 [8192, 16384], P('ch', 'ctx'), may hold values from -6 to 6
- short_taps: float32 [3, 7, 8192], P(None, None, 'ch'), may hold values from -2 to 2
- long_filter: bfloat16 [4, 2048, 16384], P('ch', 'ctx'), may hold values from -1.5 to 1.5
- skip_gain: float32 [4, 2048], P('ch', 'ctx'), may hold values from 0.5 to 1.5
Outputs:
- mixed: bfloat16 [8192, 16384], P('ch', 'ctx')
The draws below stay inside these ranges and needn't reach their ends.
All inputs are finite; a program needn't handle non-finite values.
Results may differ from the reference program's by a relative error of at most 0.01.
Values may be sent and summed in bfloat16 or wider, within the bound.
No kernel may reach another device: no remote copies, remote signals or barrier semaphores. Data moves between devices by JAX's collectives and lax.ppermute only.
A program may use at most 64 MiB of HBM per device.

```python
import math
import jax
import jax.numpy as jnp
from jax import lax

D = 8192
TAPS = 7
TOKENS = 16384
GROUPS = 4
GROUP_WIDTH = 2048


def draw_long_filter(key, part):
    key_noise, key_rate = jax.random.split(jax.random.fold_in(key, 11))
    noise = jnp.clip(jax.random.normal(key_noise, (GROUPS, GROUP_WIDTH, TOKENS), jnp.float32), -6.0, 6.0)
    low = math.log(0.5 / TOKENS)
    high = math.log(1.0 / 30.0)
    rates = jnp.exp(jax.random.uniform(key_rate, (GROUPS, GROUP_WIDTH, 1), jnp.float32, low, high))
    positions = jnp.arange(TOKENS, dtype=jnp.float32)
    scales = jnp.sqrt(1.0 - jnp.exp(-2.0 * rates))
    return (noise * scales * jnp.exp(-rates * positions)).astype(jnp.bfloat16)


def level_of(own_key, dims, cuts, smallest, high):
    def one(dim, parts):
        steps = jax.random.uniform(jax.random.fold_in(jax.random.fold_in(own_key, 6), dim), (parts,), jnp.float32, smallest / len(cuts), high / len(cuts))
        return jnp.repeat(jnp.exp(steps), dims[dim] // parts).reshape((-1,) + (1,) * (len(dims) - dim - 1))

    loudness = one(*cuts[0])
    for cut in cuts[1:]:
        loudness = loudness * one(*cut)
    return loudness


def gaussian(key, dims, width, most, cuts=(), kind=jnp.bfloat16):
    factor_of = level_of(key, dims, cuts, -0.22, 0.18) if cuts else 1.0
    result = jax.random.normal(key, dims, jnp.float32) * width * factor_of
    return jnp.minimum(jnp.maximum(result, -most), most).astype(kind)


def setup_inputs(seed: int = 0) -> dict:
    splits = jax.random.split(jax.random.key(seed), 7)
    return {
        "queries": gaussian(splits[0], (D, TOKENS), 1.0, 6.0, ((0, 4), (1, 64))),
        "keys": gaussian(splits[1], (D, TOKENS), 1.0, 6.0, ((0, 4), (1, 64))),
        "values": gaussian(splits[2], (D, TOKENS), 1.0, 6.0, ((0, 4), (1, 64))),
        "short_taps": gaussian(splits[3], (3, TAPS, D), TAPS ** -0.5, 2.0, ((2, 4),), jnp.float32),
        "long_filter": draw_long_filter(jax.random.fold_in(splits[6], 71), 0),
        "skip_gain": jnp.clip(0.5 + 1.0 * jax.random.uniform(splits[5], (GROUPS, GROUP_WIDTH), jnp.float32) ** level_of(splits[5], (GROUPS, GROUP_WIDTH), ((0, 4), (1, 64)), -0.2, 0.2), 0.5, 1.5),
    }


def short_conv(source, taps):
    rim = taps.shape[0] - 1
    length = source.shape[1]
    padded = jnp.pad(source.astype(jnp.float32), ((0, 0), (rim, 0)))
    total = jnp.zeros(source.shape, jnp.float32)
    for shift_j in range(taps.shape[0]):
        total = total + taps[shift_j][:, None] * padded[:, rim - shift_j:rim - shift_j + length]
    return total


def reference(queries, keys, values, short_taps, long_filter, skip_gain):
    q_short = short_conv(queries, short_taps[0]).astype(jnp.bfloat16)
    gated = (short_conv(keys, short_taps[1]) * short_conv(values, short_taps[2])).astype(jnp.bfloat16)
    filters = long_filter.reshape(D, TOKENS)
    skips = skip_gain.reshape(D)
    block = math.gcd(D, 512)
    count = D // block
    padded_len = 2 * TOKENS

    def one_block(pair):
        sig, filt = pair
        spec = jnp.fft.rfft(sig.astype(jnp.float32), n=padded_len, axis=1) * jnp.fft.rfft(filt.astype(jnp.float32), n=padded_len, axis=1)
        return jnp.fft.irfft(spec, n=padded_len, axis=1)[:, :TOKENS]

    conv = lax.map(one_block, (gated.reshape(count, block, TOKENS), filters.reshape(count, block, TOKENS)))
    long_out = (conv.reshape(D, TOKENS) + skips[:, None] * gated.astype(jnp.float32)).astype(jnp.bfloat16)
    return (q_short.astype(jnp.float32) * long_out.astype(jnp.float32)).astype(jnp.bfloat16)
```

```python
import functools

import jax
import jax.numpy as jnp
import numpy as np
from jax import lax
from jax.experimental import pallas as pl
from jax.experimental.pallas import tpu as pltpu
from jax.sharding import PartitionSpec as P

VMEM_LIMIT = 48 * 1024 * 1024
RIM = 8
BF16, F32 = jnp.bfloat16, jnp.float32


def head_and_rest(table):
    head = table.astype(np.float32).astype(jnp.bfloat16)
    rest = (table - head.astype(np.float64)).astype(np.float32).astype(jnp.bfloat16)
    return head, rest


def transform_tables(side, runs):
    length = side * side
    k = np.arange(side)
    natural = np.arange(side)
    blocks = side // runs
    held = (np.arange(blocks)[None, :] * runs + np.arange(runs)[:, None]).reshape(-1)

    def first(order):
        angle = 2 * np.pi * (k[:, None] + 0.25) * order[None, :] / side
        both = np.concatenate([np.cos(angle), np.sin(angle)], axis=0)
        return np.concatenate(head_and_rest(both), axis=1)

    turn = 2 * np.pi * (k[:, None] + 0.25) * natural[None, :] / length
    twist = np.stack([np.cos(turn), np.sin(turn)]).astype(np.float32)
    angle = 2 * np.pi * (natural[:, None] * k[None, :] % side) / side
    cos, sin = np.cos(angle), np.sin(angle)

    def second(matrix):
        head, rest = head_and_rest(matrix)
        return np.concatenate([head, head, rest], axis=0)

    ahead = second(np.block([[cos, sin], [-sin, cos]]))
    back = second(np.block([[cos, -sin], [sin, cos]]))
    angle = 2 * np.pi * held[:, None] * (k[None, :] + 0.25) / side
    head, rest = head_and_rest(np.concatenate([np.cos(angle), np.sin(angle)], axis=1) / length)
    last = np.concatenate([head, head, rest], axis=1)
    return first(natural), first(held), twist, ahead, back, last


def split(array):
    head = array.astype(BF16)
    return head, (array - head.astype(F32)).astype(BF16)


def dot(a, b):
    return jnp.dot(a, b, preferred_element_type=F32)


def tail_kernel(k_ref, v_ref, q_ref, out_ref):
    parts = [ref[...].astype(F32).T[-RIM:] for ref in (k_ref, v_ref, q_ref)]
    parts.append(jnp.zeros_like(parts[0]))
    out_ref[...] = jnp.concatenate(parts, axis=0).astype(BF16)


def short_conv(source, halo, taps_ref, which, ext):
    count = source.shape[1]
    ext[:RIM] = halo
    ext[RIM:] = source.astype(F32).T
    total = taps_ref[which, 0:1] * ext[RIM : RIM + count]
    for j in range(1, taps_ref.shape[1]):
        total = total + taps_ref[which, j : j + 1] * ext[RIM - j : RIM - j + count]
    return total


def gate_kernel(k_ref, v_ref, halo_ref, taps_ref, out_ref, k_ext, v_ext):
    halo = halo_ref[...].astype(F32)
    keys = short_conv(k_ref[...], halo[:RIM], taps_ref, 1, k_ext)
    values = short_conv(v_ref[...], halo[RIM : 2 * RIM], taps_ref, 2, v_ext)
    out_ref[...] = (keys * values).T.astype(BF16)


def query_kernel(q_ref, halo_ref, taps_ref, out_ref, q_ext):
    halo = halo_ref[...].astype(F32)
    queries = short_conv(q_ref[...], halo[2 * RIM : 3 * RIM], taps_ref, 0, q_ext)
    out_ref[...] = queries.T.astype(BF16)


def to_spectrum(pairs, first, twist, ahead):
    side = twist.shape[1]
    cos, sin = twist[0], twist[1]
    stacked = []
    for pair in pairs:
        both = dot(first, jnp.concatenate([pair, pair], axis=0))
        for i in range(2):
            re = both[:side, i * side : (i + 1) * side]
            im = both[side:, i * side : (i + 1) * side]
            turned = jnp.concatenate([re * cos - im * sin, re * sin + im * cos], axis=1)
            head, rest = split(turned)
            stacked.append(jnp.concatenate([head, rest, head], axis=1))
    return dot(jnp.concatenate(stacked, axis=0), ahead)


def filter_kernel(filt_ref, gain_ref, first_ref, twist_ref, ahead_ref, out_ref):
    count, side, _ = filt_ref.shape
    pairs = [
        jnp.concatenate([filt_ref[c], filt_ref[c + 1]], axis=1) for c in range(0, count, 2)
    ]
    spectrum = to_spectrum(pairs, first_ref[...], twist_ref, ahead_ref[...])
    base = pl.program_id(0) * count
    for c in range(count):
        rows = spectrum[c * side : (c + 1) * side]
        re, im = rows[:, :side] + gain_ref[0, base + c], rows[:, side:]
        out_ref[c] = jnp.concatenate([re, im], axis=1)


def long_kernel(
    x_ref, filt_ref, first_ref, twist_ref, ahead_ref, back_ref, last_ref, out_ref, x_wide, y_wide
):
    blocks, owned, width = x_ref.shape
    count, side, _ = filt_ref.shape
    step = pl.program_id(0)

    @pl.when(step == 0)
    def _():
        for i in range(x_wide.shape[0]):
            piece = x_ref[:, :, i * side : (i + 1) * side]
            x_wide[i] = piece.astype(F32).reshape(blocks * owned, side)

    cos, sin = twist_ref[0], twist_ref[1]
    runs = width // side
    held = []
    for c in range(count):
        rows = [
            x_wide[i, pl.ds(step * count + c, blocks, stride=owned), :] for i in range(runs)
        ]
        held.append(jnp.concatenate(rows, axis=0).astype(BF16))
    pairs = [jnp.concatenate(held[c : c + 2], axis=1) for c in range(0, count, 2)]
    spectrum = to_spectrum(pairs, first_ref[...], twist_ref, ahead_ref[...])
    stacked = []
    for c in range(count):
        rows = spectrum[c * side : (c + 1) * side]
        re, im = rows[:, :side], rows[:, side:]
        fre, fim = filt_ref[c, :, :side], filt_ref[c, :, side:]
        head, rest = split(jnp.concatenate([re * fre - im * fim, re * fim + im * fre], axis=1))
        stacked.append(jnp.concatenate([head, rest, head], axis=1))
    undone = dot(jnp.concatenate(stacked, axis=0), back_ref[...])
    for c in range(0, count, 2):
        columns = []
        for i in (c, c + 1):
            rows = undone[i * side : (i + 1) * side]
            re, im = rows[:, :side], rows[:, side:]
            turned = jnp.concatenate([re * cos + im * sin, im * cos - re * sin], axis=0)
            head, rest = split(turned)
            columns.append(jnp.concatenate([head, rest, head], axis=0))
        result = dot(last_ref[...], jnp.concatenate(columns, axis=1))
        for i in range(2):
            for j in range(runs):
                y_wide[j, pl.ds(step * count + c + i, blocks, stride=owned), :] = result[
                    j * blocks : (j + 1) * blocks, i * side : (i + 1) * side
                ]

    @pl.when(step == pl.num_programs(0) - 1)
    def _():
        for j in range(runs):
            out_ref[:, :, j * side : (j + 1) * side] = (
                y_wide[j].astype(BF16).reshape(blocks, owned, side)
            )


def params():
    return pltpu.CompilerParams(vmem_limit_bytes=VMEM_LIMIT)


def local(queries, keys, values, short_taps, long_filter, skip_gain):
    ctx_count = lax.axis_size("ctx")
    width, tokens = queries.shape
    owned = width // ctx_count
    side = 128
    runs = tokens // side
    first_plain, first_held, twist, ahead, back, last = (
        jnp.asarray(t) for t in transform_tables(side, runs)
    )
    n_taps = short_taps.shape[1]

    rows = 512
    tail_spec = pl.BlockSpec((rows, 128), lambda i: (i, tokens // 128 - 1))
    with jax.named_scope("tail"):
        tail = pl.pallas_call(
            tail_kernel,
            grid=(width // rows,),
            in_specs=[tail_spec] * 3,
            out_specs=pl.BlockSpec((4 * RIM, rows), lambda i: (0, i)),
            out_shape=jax.ShapeDtypeStruct((4 * RIM, width), BF16),
            compiler_params=params(),
        )(keys, values, queries)
    halo = lax.ppermute(tail, "ctx", [(i, i + 1) for i in range(ctx_count - 1)])

    rows = 256
    data_spec = pl.BlockSpec((rows, tokens), lambda i: (i, 0))
    halo_spec = pl.BlockSpec((4 * RIM, rows), lambda i: (0, i))
    taps_spec = pl.BlockSpec((3, n_taps, rows), lambda i: (0, 0, i))
    ext = pltpu.VMEM((RIM + tokens, rows), F32)
    with jax.named_scope("gate"):
        gated = pl.pallas_call(
            gate_kernel,
            grid=(width // rows,),
            in_specs=[data_spec, data_spec, halo_spec, taps_spec],
            out_specs=data_spec,
            out_shape=jax.ShapeDtypeStruct((width, tokens), BF16),
            scratch_shapes=[ext, ext],
            compiler_params=params(),
            cost_estimate=pl.CostEstimate(
                flops=30 * width * tokens, bytes_accessed=6 * width * tokens, transcendentals=0
            ),
        )(keys, values, halo, short_taps)
    arrived = lax.all_to_all(
        gated.reshape(ctx_count, owned, tokens), "ctx", split_axis=0, concat_axis=0, tiled=True
    )
    with jax.named_scope("query"):
        q_short = pl.pallas_call(
            query_kernel,
            grid=(width // rows,),
            in_specs=[data_spec, halo_spec, taps_spec],
            out_specs=data_spec,
            out_shape=jax.ShapeDtypeStruct((width, tokens), BF16),
            scratch_shapes=[ext],
            compiler_params=params(),
            cost_estimate=pl.CostEstimate(
                flops=15 * width * tokens, bytes_accessed=4 * width * tokens, transcendentals=0
            ),
        )(queries, halo, short_taps)

    count = 4
    whole = pl.BlockSpec(memory_space=pltpu.VMEM)
    spectrum_spec = pl.BlockSpec((count, side, 2 * side), lambda i: (i, 0, 0))
    with jax.named_scope("filter"):
        spectrum = pl.pallas_call(
            filter_kernel,
            grid=(owned // count,),
            in_specs=[
                pl.BlockSpec((count, side, side), lambda i: (i, 0, 0)),
                pl.BlockSpec(memory_space=pltpu.SMEM),
                whole,
                whole,
                whole,
            ],
            out_specs=spectrum_spec,
            out_shape=jax.ShapeDtypeStruct((owned, side, 2 * side), F32),
            compiler_params=params(),
            cost_estimate=pl.CostEstimate(
                flops=owned * side * side * side * 16, bytes_accessed=5 << 20, transcendentals=0
            ),
        )(long_filter.reshape(owned, side, side), skip_gain, first_plain, twist, ahead)
    wide = pltpu.VMEM((runs, ctx_count * owned, side), F32)
    with jax.named_scope("long"):
        long = pl.pallas_call(
            long_kernel,
            grid=(owned // count,),
            in_specs=[whole, spectrum_spec, whole, whole, whole, whole, whole],
            out_specs=pl.BlockSpec((ctx_count, owned, tokens), lambda i: (0, 0, 0)),
            out_shape=jax.ShapeDtypeStruct((ctx_count, owned, tokens), BF16),
            scratch_shapes=[wide, wide],
            compiler_params=params(),
            cost_estimate=pl.CostEstimate(
                flops=owned * side * side * side * 32, bytes_accessed=7 << 20, transcendentals=0
            ),
        )(arrived, spectrum, first_held, twist, ahead, back, last)
    returned = lax.all_to_all(long, "ctx", split_axis=0, concat_axis=0, tiled=True)
    returned = returned.reshape(width, tokens)
    return (q_short.astype(F32) * returned.astype(F32)).astype(BF16)


def solution(mesh):
    placed = (
        P("ch", "ctx"),
        P("ch", "ctx"),
        P("ch", "ctx"),
        P(None, None, "ch"),
        P("ch", "ctx", None),
        P("ch", "ctx"),
    )
    return jax.shard_map(
        local, mesh=mesh, in_specs=placed, out_specs=P("ch", "ctx"), check_vma=False
    )
```

```python
import jax
import jax.numpy as jnp
import numpy as np
from jax import lax
from jax.experimental import pallas as pl
from jax.experimental.pallas import tpu as pltpu
from jax.sharding import PartitionSpec as P

VMEM_LIMIT = 24 * 1024 * 1024
VMEM_FILTER = 60 * 1024 * 1024
VMEM_SOME = 52 * 1024 * 1024
VMEM_MOST = 63 * 1024 * 1024
RIM = 8
TAPS = 7
GROUP = 8
BF16, F32 = jnp.bfloat16, jnp.float32


def head_and_rest(table):
    head = table.astype(np.float32).astype(jnp.bfloat16)
    rest = (table - head.astype(np.float64)).astype(np.float32).astype(jnp.bfloat16)
    return head, rest


def transform_tables(side, runs):
    length = side * side
    k = np.arange(side)
    natural = np.arange(side)
    blocks = side // runs
    held = (np.arange(blocks)[None, :] * runs + np.arange(runs)[:, None]).reshape(-1)

    def first(order):
        angle = 2 * np.pi * (k[:, None] + 0.25) * order[None, :] / side
        both = np.concatenate([np.cos(angle), np.sin(angle)], axis=0)
        return np.concatenate(head_and_rest(both), axis=1)

    turn = 2 * np.pi * (k[:, None] + 0.25) * natural[None, :] / length
    twist = np.stack([np.cos(turn), np.sin(turn)]).astype(np.float32)
    angle = 2 * np.pi * (natural[:, None] * k[None, :] % side) / side
    cos, sin = np.cos(angle), np.sin(angle)

    def second(matrix):
        head, rest = head_and_rest(matrix)
        return np.concatenate([head, head, rest], axis=0)

    ahead = second(np.block([[cos, sin], [-sin, cos]]))
    back = second(np.block([[cos, -sin], [sin, cos]]))
    angle = 2 * np.pi * held[:, None] * (k[None, :] + 0.25) / side
    head, rest = head_and_rest(np.concatenate([np.cos(angle), np.sin(angle)], axis=1) / length)
    last = np.concatenate([head, head, rest], axis=1)
    return first(natural), first(held), twist, ahead, back, last


def split(array):
    head = array.astype(BF16)
    return head, (array - head.astype(F32)).astype(BF16)


def dot(a, b):
    return jnp.dot(a, b, preferred_element_type=F32)


def fetch(source, target, sems, columns):
    rows = target.shape[0] // sems.shape[0]
    copies = []
    for i in range(sems.shape[0]):
        cut = pl.ds(i * rows, rows)
        copies.append(
            pltpu.make_async_copy(source.at[cut, columns], target.at[cut], sems.at[i])
        )
        copies[-1].start()
    return copies


def tail_kernel(q_ref, out_ref, held, sems):
    copies = fetch(q_ref, held, sems, pl.ds(q_ref.shape[1] - 128, 128))
    rows = held.shape[0] // len(copies)
    for i, copy in enumerate(copies):
        copy.wait()
        out_ref[:, i * rows : (i + 1) * rows] = held[i * rows : (i + 1) * rows].T[-2 * RIM :]


def short_conv(block, halo, taps_ref, which, c0, ext):
    count = block.shape[0]
    ext[:RIM] = halo
    ext[RIM:] = block
    channels = pl.ds(c0, 128)
    total = taps_ref[which, 0:1, channels] * block
    for j in range(1, taps_ref.shape[1]):
        total = total + taps_ref[which, j : j + 1, channels] * ext[RIM - j : RIM - j + count]
    return total


def gate_kernel(
    k_ref, v_ref, far_ref, out_ref, ext, held, done, taps_ref, sems_in, sems_out, sem_taps
):
    width, tokens = k_ref.shape
    runs = tokens // 128
    owned = width // out_ref.shape[0]
    fit = 128 // owned
    chunks = sems_out.shape[0]
    rows = width // chunks
    lane = lax.broadcasted_iota(jnp.int32, (RIM, 128), 1) // owned
    nothing = jnp.zeros((RIM, 128), F32)
    turn = lax.axis_index("ctx") % fit

    def fetch(i):
        cut = pl.ds(i * rows, rows)
        for n, ref in enumerate((k_ref, v_ref)):
            yield pltpu.make_async_copy(ref.at[cut], held.at[n, cut], sems_in.at[n, i])

    def send(i):
        cut = pl.ds(i * rows // owned, rows // owned)
        return pltpu.make_async_copy(done.at[cut], out_ref.at[cut], sems_out.at[i])

    taps_copy = pltpu.make_async_copy(far_ref, taps_ref, sem_taps)
    taps_copy.start()
    for i in range(chunks):
        for copy in fetch(i):
            copy.start()
    taps_copy.wait()
    for i in range(chunks):
        for copy in fetch(i):
            copy.wait()
        for c in range(i * rows, (i + 1) * rows, 128):
            both, rims = [], []
            for n in range(2):
                turned = held[n, c : c + 128].T.astype(F32)
                both.append(short_conv(turned, nothing, taps_ref, n + 1, c, ext.at[n]))
                rims.append((turned[tokens - RIM :], turned[:RIM]))
            gated = (both[0] * both[1]).astype(BF16)
            first = c // owned
            for j in range(runs):
                piece = gated[j * 128 : (j + 1) * 128].T
                done[first : first + fit, j * owned : (j + 1) * owned] = piece.reshape(fit, owned, 128)
            sides = (rims[0][1], rims[0][0], rims[1][1], rims[1][0])
            for d in range(fit):
                rim = nothing
                for g, side in enumerate(sides):
                    moved = pltpu.roll(side, (g - d) % fit * owned, 1)
                    rim = jnp.where(lane == g, moved, rim)
                rim = pltpu.roll(rim, turn * owned, 1)
                done[first + d, runs * owned :] = rim.astype(BF16)
        send(i).start()
    for i in range(chunks):
        send(i).wait()


def query_kernel(q_ref, halo_ref, taps_ref, out_ref, ext):
    width = q_ref.shape[0]
    for c in range(0, width, 128):
        halo = halo_ref[:, c : c + 128].astype(F32)
        turned = q_ref[c : c + 128].T.astype(F32)
        queries = short_conv(turned, halo[RIM:], taps_ref, 0, c, ext)
        out_ref[c : c + 128] = queries.astype(BF16).T


def to_spectrum(pairs, first, twist, ahead):
    side = twist.shape[1]
    cos, sin = twist[0], twist[1]
    stacked = []
    for pair in pairs:
        both = dot(first, jnp.concatenate([pair, pair], axis=0))
        for i in range(2):
            re = both[:side, i * side : (i + 1) * side]
            im = both[side:, i * side : (i + 1) * side]
            turned = jnp.concatenate([re * cos - im * sin, re * sin + im * cos], axis=1)
            head, rest = split(turned)
            stacked.append(dot(jnp.concatenate([head, rest, head], axis=1), ahead))
    return stacked


def filter_kernel(
    filt_ref, gain_ref, first_ref, twist_ref, ahead_ref, out_ref, done, sems
):
    owned, side, _ = filt_ref.shape

    def send(step):
        cut = pl.ds(step * GROUP, GROUP)
        return pltpu.make_async_copy(done.at[cut], out_ref.at[cut], sems.at[step])

    @pl.loop(0, owned // GROUP)
    def _(step):
        base = step * GROUP
        pairs = [
            jnp.concatenate([filt_ref[base + c], filt_ref[base + c + 1]], axis=1)
            for c in range(0, GROUP, 2)
        ]
        spectrum = to_spectrum(pairs, first_ref[...], twist_ref, ahead_ref[...])
        for c, rows in enumerate(spectrum):
            re, im = rows[:, :side] + gain_ref[0, base + c], rows[:, side:]
            done[base + c] = jnp.concatenate([re, im], axis=1)
        send(step).start()

    for step in range(owned // GROUP):
        send(step).wait()


def first_tokens(x_ref, taps_ref, x_wide, ext, owned):
    blocks, rows, lanes = x_ref.shape
    fit = lanes // owned
    steps = blocks // fit
    rims = x_ref[:, rows - RIM :].astype(F32)
    before = jnp.concatenate([jnp.zeros((1, RIM, lanes), F32), rims[:-1]], axis=0)
    group = lax.broadcasted_iota(jnp.int32, (RIM, lanes), 1) // owned
    for q in range(steps):
        for n in range(2):
            for start, source in ((0, before), (RIM, rims)):
                packed = source[q * fit]
                for i in range(1, fit):
                    packed = jnp.where(group == (i + 2 * n) % fit, source[q * fit + i], packed)
                ext[n, q, start : start + RIM] = packed
    sums = []
    for n in range(2):
        total = taps_ref[RIM * n : RIM * n + 1] * ext[n, :, RIM:]
        for j in range(1, TAPS):
            tap = taps_ref[RIM * n + j : RIM * n + j + 1]
            total = total + tap * ext[n, :, RIM - j : 2 * RIM - j]
        sums.append(total)
    for q in range(steps):
        gated = sums[0][q] * pltpu.roll(sums[1][q], 2 * owned, 1)
        x_wide[0, q * lanes : (q + 1) * lanes, :RIM] = gated.T.astype(BF16).astype(F32)


def long_kernel(
    x_ref, far_ref, taps_ref, first_ref, twist_ref, ahead_ref, back_ref, last_ref, out_ref,
    x_wide, y_wide, filt_ref, ext, done, sems, sems_in,
):
    blocks, owned, width = out_ref.shape
    side = filt_ref.shape[1]

    def fetched(step):
        cut = pl.ds(step * GROUP, GROUP)
        return pltpu.make_async_copy(far_ref.at[cut], filt_ref.at[cut], sems_in.at[step])

    for step in range(owned // GROUP):
        fetched(step).start()
    runs = width // side
    for j in range(runs):
        piece = x_ref[:, j * owned : (j + 1) * owned]
        x_wide[j] = piece.astype(F32).reshape(blocks * owned, side)
    first_tokens(x_ref, taps_ref, x_wide, ext, owned)
    cos, sin = twist_ref[0], twist_ref[1]

    def some(base):
        held = []
        for c in range(GROUP):
            rows = [x_wide[j, pl.ds(base + c, blocks, stride=owned), :] for j in range(runs)]
            held.append(jnp.concatenate(rows, axis=0).astype(BF16))
        pairs = [jnp.concatenate(held[c : c + 2], axis=1) for c in range(0, GROUP, 2)]
        spectrum = to_spectrum(pairs, first_ref[...], twist_ref, ahead_ref[...])
        undone = []
        for c, rows in enumerate(spectrum):
            re, im = rows[:, :side], rows[:, side:]
            both = filt_ref[base + c]
            fre, fim = both[:, :side], both[:, side:]
            head, rest = split(jnp.concatenate([re * fre - im * fim, re * fim + im * fre], axis=1))
            undone.append(dot(jnp.concatenate([head, rest, head], axis=1), back_ref[...]))
        for c in range(0, GROUP, 2):
            columns = []
            for rows in undone[c : c + 2]:
                re, im = rows[:, :side], rows[:, side:]
                turned = jnp.concatenate([re * cos + im * sin, im * cos - re * sin], axis=0)
                head, rest = split(turned)
                columns.append(jnp.concatenate([head, rest, head], axis=0))
            result = dot(last_ref[...], jnp.concatenate(columns, axis=1))
            for i in range(2):
                for j in range(runs):
                    y_wide[j, pl.ds(base + c + i, blocks, stride=owned), :] = result[
                        j * blocks : (j + 1) * blocks, i * side : (i + 1) * side
                    ]

    part = owned // sems.shape[0]
    copies = []
    for h in range(sems.shape[0]):

        @pl.loop(0, part // GROUP)
        def _(step, h=h):
            fetched(h * (part // GROUP) + step).wait()
            some(h * part + step * GROUP)

        for j in range(runs):
            whole = y_wide[j].reshape(blocks, owned, side)
            done[h, :, :, j * side : (j + 1) * side] = (
                whole[:, h * part : (h + 1) * part].astype(BF16)
            )
        copies.append(
            pltpu.make_async_copy(done.at[h], out_ref.at[:, pl.ds(h * part, part)], sems.at[h])
        )
        copies[-1].start()
    for copy in copies:
        copy.wait()


def product_kernel(q_ref, long_ref, out_ref, done, sems):
    chunks = sems.shape[0]
    rows = done.shape[0] // chunks
    copies = []
    for i in range(chunks):
        cut = pl.ds(i * rows, rows)
        done[cut] = (q_ref[cut].astype(F32) * long_ref[cut].astype(F32)).astype(BF16)
        copies.append(pltpu.make_async_copy(done.at[cut], out_ref.at[cut], sems.at[i]))
        copies[-1].start()
    for copy in copies:
        copy.wait()


def cost(flops, size):
    return pl.CostEstimate(flops=flops, bytes_accessed=size, transcendentals=0)


def params(limit=VMEM_LIMIT):
    return pltpu.CompilerParams(vmem_limit_bytes=limit)


def local(queries, keys, values, short_taps, long_filter, skip_gain):
    ctx_count = lax.axis_size("ctx")
    width, tokens = queries.shape
    owned = width // ctx_count
    side = 128
    runs = tokens // side
    first_plain, first_held, twist, ahead, back, last = (
        jnp.asarray(t) for t in transform_tables(side, runs)
    )

    far = pl.BlockSpec(memory_space=pltpu.HBM)
    whole = pl.BlockSpec(memory_space=pltpu.VMEM)
    shift = [(i, i + 1) for i in range(ctx_count - 1)]

    shape = jax.ShapeDtypeStruct((width, tokens), BF16)
    chunks = 8
    held_rows = runs * owned + RIM
    with jax.named_scope("gate"):
        gated = pl.pallas_call(
            gate_kernel,
            in_specs=[far, far, far],
            out_specs=far,
            out_shape=jax.ShapeDtypeStruct((ctx_count, held_rows, side), BF16),
            scratch_shapes=[
                pltpu.VMEM((2, RIM + tokens, 128), F32),
                pltpu.VMEM((2, width, tokens), BF16),
                pltpu.VMEM((ctx_count, held_rows, side), BF16),
                pltpu.VMEM(short_taps.shape, F32),
                pltpu.SemaphoreType.DMA((2, chunks)),
                pltpu.SemaphoreType.DMA((chunks,)),
                pltpu.SemaphoreType.DMA,
            ],
            compiler_params=params(VMEM_MOST),
            cost_estimate=cost(30 * width * tokens, 6 * width * tokens),
        )(keys, values, short_taps)
    arrived = lax.all_to_all(gated, "ctx", split_axis=0, concat_axis=0, tiled=True)
    own_taps = lax.dynamic_slice_in_dim(short_taps, lax.axis_index("ctx") * owned, owned, 2)
    own_taps = jnp.pad(own_taps[1:], ((0, 0), (0, RIM - TAPS), (0, 0))).reshape(2 * RIM, owned)
    own_taps = jnp.tile(own_taps, (1, side // owned))
    later_queries, _ = lax.optimization_barrier((queries, gated))
    with jax.named_scope("query_tail"):
        query_tail = pl.pallas_call(
            tail_kernel,
            in_specs=[far],
            out_specs=whole,
            out_shape=jax.ShapeDtypeStruct((2 * RIM, width), BF16),
            scratch_shapes=[pltpu.VMEM((width, 128), BF16), pltpu.SemaphoreType.DMA((4,))],
            compiler_params=params(),
            cost_estimate=cost(width * 128, 2 * width * 128),
        )(later_queries)
    query_halo = lax.ppermute(query_tail, "ctx", shift)
    with jax.named_scope("filter"):
        spectrum = pl.pallas_call(
            filter_kernel,
            in_specs=[whole, pl.BlockSpec(memory_space=pltpu.SMEM), whole, whole, whole],
            out_specs=far,
            out_shape=jax.ShapeDtypeStruct((owned, side, 2 * side), F32),
            scratch_shapes=[
                pltpu.VMEM((owned, side, 2 * side), F32),
                pltpu.SemaphoreType.DMA((owned // GROUP,)),
            ],
            compiler_params=params(VMEM_FILTER),
            cost_estimate=cost(owned * side**3 * 16, 5 << 20),
        )(long_filter.reshape(owned, side, side), skip_gain, first_plain, twist, ahead)
    spectrum, query_halo = lax.optimization_barrier((spectrum, query_halo))
    with jax.named_scope("query"):
        q_short = pl.pallas_call(
            query_kernel,
            in_specs=[whole] * 3,
            out_specs=whole,
            out_shape=shape,
            scratch_shapes=[pltpu.VMEM((RIM + tokens, 128), F32)],
            compiler_params=params(),
            cost_estimate=cost(15 * width * tokens, 4 * width * tokens),
        )(later_queries, query_halo, short_taps)
    wide = pltpu.VMEM((runs, ctx_count * owned, side), F32)
    parts = 2
    with jax.named_scope("long"):
        long = pl.pallas_call(
            long_kernel,
            in_specs=[whole, far] + [whole] * 6,
            out_specs=far,
            out_shape=jax.ShapeDtypeStruct((ctx_count, owned, tokens), BF16),
            scratch_shapes=[
                wide,
                wide,
                pltpu.VMEM((owned, side, 2 * side), F32),
                pltpu.VMEM((2, ctx_count * owned // side, 2 * RIM, side), F32),
                pltpu.VMEM((parts, ctx_count, owned // parts, tokens), BF16),
                pltpu.SemaphoreType.DMA((parts,)),
                pltpu.SemaphoreType.DMA((owned // GROUP,)),
            ],
            compiler_params=params(VMEM_SOME),
            cost_estimate=cost(owned * side**3 * 32, 7 << 20),
        )(arrived, spectrum, own_taps, first_held, twist, ahead, back, last)
    returned = lax.all_to_all(long, "ctx", split_axis=0, concat_axis=0, tiled=True)
    returned = returned.reshape(width, tokens)
    with jax.named_scope("product"):
        return pl.pallas_call(
            product_kernel,
            in_specs=[whole, whole],
            out_specs=far,
            out_shape=shape,
            scratch_shapes=[pltpu.VMEM((width, tokens), BF16), pltpu.SemaphoreType.DMA((8,))],
            compiler_params=params(),
            cost_estimate=cost(width * tokens, 6 * width * tokens),
        )(q_short, returned)


def solution(mesh):
    placed = (
        P("ch", "ctx"),
        P("ch", "ctx"),
        P("ch", "ctx"),
        P(None, None, "ch"),
        P("ch", "ctx", None),
        P("ch", "ctx"),
    )
    return jax.shard_map(
        local, mesh=mesh, in_specs=placed, out_specs=P("ch", "ctx"), check_vma=False
    )
```

```python
import jax
import jax.numpy as jnp
import numpy as np
from jax import lax
from jax.experimental import pallas as pl
from jax.experimental.pallas import tpu as pltpu
from jax.sharding import PartitionSpec as P

VMEM_LIMIT = 24 * 1024 * 1024
VMEM_FILTER = 60 * 1024 * 1024
VMEM_SOME = 52 * 1024 * 1024
VMEM_MOST = 63 * 1024 * 1024
RIM = 8
TAPS = 7
GROUP = 16
PIECE = 8
BF16, F32 = jnp.bfloat16, jnp.float32


def head_and_rest(table):
    head = table.astype(np.float32).astype(jnp.bfloat16)
    rest = (table - head.astype(np.float64)).astype(np.float32).astype(jnp.bfloat16)
    return head, rest


def transform_tables(side, runs):
    length = side * side
    k = np.arange(side)
    natural = np.arange(side)
    blocks = side // runs
    held = (np.arange(blocks)[None, :] * runs + np.arange(runs)[:, None]).reshape(-1)

    def first(order):
        angle = 2 * np.pi * (k[:, None] + 0.25) * order[None, :] / side
        both = np.concatenate([np.cos(angle), np.sin(angle)], axis=0)
        return np.concatenate(head_and_rest(both), axis=1)

    turn = 2 * np.pi * (k[:, None] + 0.25) * natural[None, :] / length
    twist = np.stack([np.cos(turn), np.sin(turn)]).astype(np.float32)
    angle = 2 * np.pi * (natural[:, None] * k[None, :] % side) / side
    cos, sin = np.cos(angle), np.sin(angle)

    def second(matrix):
        head, rest = head_and_rest(matrix)
        return np.concatenate([head, head, rest], axis=0)

    ahead = second(np.block([[cos, sin], [-sin, cos]]))
    back = second(np.block([[cos, -sin], [sin, cos]]))
    angle = 2 * np.pi * held[:, None] * (k[None, :] + 0.25) / side
    head, rest = head_and_rest(np.concatenate([np.cos(angle), np.sin(angle)], axis=1) / length)
    last = np.concatenate([head, head, rest], axis=1)
    return first(natural), first(held), twist, ahead, back, last


def split(array):
    head = array.astype(BF16)
    return head, (array - head.astype(F32)).astype(BF16)


def dot(a, b):
    return jnp.dot(a, b, preferred_element_type=F32)


def fetch(source, target, sems, columns):
    rows = target.shape[0] // sems.shape[0]
    copies = []
    for i in range(sems.shape[0]):
        cut = pl.ds(i * rows, rows)
        copies.append(
            pltpu.make_async_copy(source.at[cut, columns], target.at[cut], sems.at[i])
        )
        copies[-1].start()
    return copies


def tail_kernel(q_ref, out_ref, held, sems):
    copies = fetch(q_ref, held, sems, pl.ds(q_ref.shape[1] - 128, 128))
    rows = held.shape[0] // len(copies)
    for i, copy in enumerate(copies):
        copy.wait()
        out_ref[:, i * rows : (i + 1) * rows] = held[i * rows : (i + 1) * rows].T[-2 * RIM :]


def short_conv(block, halo, taps_ref, which, c0, ext):
    count = block.shape[0]
    ext[:RIM] = halo
    ext[RIM:] = block
    channels = pl.ds(c0, 128)
    total = taps_ref[which, 0:1, channels] * block
    for j in range(1, taps_ref.shape[1]):
        total = total + taps_ref[which, j : j + 1, channels] * ext[RIM - j : RIM - j + count]
    return total


def gate_kernel(
    k_ref, v_ref, far_ref, out_ref, ext, held, done, taps_ref, sems_in, sems_out, sem_taps
):
    width, tokens = k_ref.shape
    runs = tokens // 128
    owned = width // out_ref.shape[0]
    fit = 128 // owned
    chunks = sems_out.shape[0]
    rows = width // chunks
    lane = lax.broadcasted_iota(jnp.int32, (RIM, 128), 1) // owned
    nothing = jnp.zeros((RIM, 128), F32)
    turn = lax.axis_index("ctx") % fit

    def fetch(i):
        cut = pl.ds(i * rows, rows)
        for n, ref in enumerate((k_ref, v_ref)):
            yield pltpu.make_async_copy(ref.at[cut], held.at[n, cut], sems_in.at[n, i])

    def send(i):
        cut = pl.ds(i * rows // owned, rows // owned)
        return pltpu.make_async_copy(done.at[cut], out_ref.at[cut], sems_out.at[i])

    taps_copy = pltpu.make_async_copy(far_ref, taps_ref, sem_taps)
    taps_copy.start()
    for i in range(chunks):
        for copy in fetch(i):
            copy.start()
    taps_copy.wait()
    for i in range(chunks):
        for copy in fetch(i):
            copy.wait()
        for c in range(i * rows, (i + 1) * rows, 128):
            both, rims = [], []
            for n in range(2):
                turned = held[n, c : c + 128].T.astype(F32)
                rows_ext = ext.at[c // 128 % ext.shape[0], n]
                both.append(short_conv(turned, nothing, taps_ref, n + 1, c, rows_ext))
                rims.append((turned[tokens - RIM :], turned[:RIM]))
            gated = (both[0] * both[1]).astype(BF16)
            first = c // owned
            for j in range(runs):
                piece = gated[j * 128 : (j + 1) * 128].T
                done[first : first + fit, j * owned : (j + 1) * owned] = piece.reshape(fit, owned, 128)
            sides = (rims[0][1], rims[0][0], rims[1][1], rims[1][0])
            for d in range(fit):
                rim = nothing
                for g, side in enumerate(sides):
                    moved = pltpu.roll(side, (g - d) % fit * owned, 1)
                    rim = jnp.where(lane == g, moved, rim)
                rim = pltpu.roll(rim, turn * owned, 1)
                done[first + d, runs * owned :] = rim.astype(BF16)
        send(i).start()
    for i in range(chunks):
        send(i).wait()


def query_kernel(q_ref, halo_ref, taps_ref, out_ref, ext):
    width = q_ref.shape[0]
    for c in range(0, width, 128):
        halo = halo_ref[:, c : c + 128].astype(F32)
        turned = q_ref[c : c + 128].T.astype(F32)
        queries = short_conv(turned, halo[RIM:], taps_ref, 0, c, ext)
        out_ref[c : c + 128] = queries.astype(BF16).T


def enter_pair(pair, first, cos, sin):
    side = pair.shape[0]
    both = dot(first, jnp.concatenate([pair, pair], axis=0))
    parts = []
    for i in range(2):
        re = both[:side, i * side : (i + 1) * side]
        im = both[side:, i * side : (i + 1) * side]
        turned = jnp.concatenate([re * cos - im * sin, re * sin + im * cos], axis=1)
        head, rest = split(turned)
        parts.append(jnp.concatenate([head, rest, head], axis=1))
    return parts


def to_spectrum(pairs, first, twist, ahead):
    return [
        dot(part, ahead) for pair in pairs for part in enter_pair(pair, first, twist[0], twist[1])
    ]


def filter_kernel(
    filt_ref, gain_ref, first_ref, twist_ref, ahead_ref, out_ref, done, sems
):
    owned, side, _ = filt_ref.shape

    def send(step):
        cut = pl.ds(step * PIECE, PIECE)
        return pltpu.make_async_copy(done.at[cut], out_ref.at[cut], sems.at[step])

    @pl.loop(0, owned // PIECE)
    def _(step):
        base = step * PIECE
        pairs = [
            jnp.concatenate([filt_ref[base + c], filt_ref[base + c + 1]], axis=1)
            for c in range(0, PIECE, 2)
        ]
        spectrum = to_spectrum(pairs, first_ref[...], twist_ref, ahead_ref[...])
        for c, rows in enumerate(spectrum):
            re, im = rows[:, :side] + gain_ref[0, base + c], rows[:, side:]
            done[base + c] = jnp.concatenate([re, im], axis=1)
        send(step).start()

    for step in range(owned // PIECE):
        send(step).wait()


def first_tokens(x_ref, taps_ref, x_wide, ext, owned):
    blocks, rows, lanes = x_ref.shape
    fit = lanes // owned
    steps = blocks // fit
    rims = x_ref[:, rows - RIM :].astype(F32)
    before = jnp.concatenate([jnp.zeros((1, RIM, lanes), F32), rims[:-1]], axis=0)
    group = lax.broadcasted_iota(jnp.int32, (RIM, lanes), 1) // owned
    for q in range(steps):
        for n in range(2):
            for start, source in ((0, before), (RIM, rims)):
                packed = source[q * fit]
                for i in range(1, fit):
                    packed = jnp.where(group == (i + 2 * n) % fit, source[q * fit + i], packed)
                ext[n, q, start : start + RIM] = packed
    sums = []
    for n in range(2):
        total = taps_ref[RIM * n : RIM * n + 1] * ext[n, :, RIM:]
        for j in range(1, TAPS):
            tap = taps_ref[RIM * n + j : RIM * n + j + 1]
            total = total + tap * ext[n, :, RIM - j : 2 * RIM - j]
        sums.append(total)
    for q in range(steps):
        gated = sums[0][q] * pltpu.roll(sums[1][q], 2 * owned, 1)
        x_wide[0, q * lanes : (q + 1) * lanes, :RIM] = gated.T.astype(BF16).astype(F32)


def long_kernel(
    x_ref, far_ref, far_taps_ref, first_ref, twist_ref, ahead_ref, back_ref, last_ref, out_ref,
    x_wide, y_wide, filt_ref, taps_ref, ext, done, sems, sems_in, sem_taps,
):
    blocks, owned, width = out_ref.shape
    side = filt_ref.shape[1]

    def fetched(piece):
        cut = pl.ds(piece * PIECE, PIECE)
        return pltpu.make_async_copy(far_ref.at[cut], filt_ref.at[cut], sems_in.at[piece])

    taps_copy = pltpu.make_async_copy(far_taps_ref, taps_ref, sem_taps)
    taps_copy.start()
    fetched(0).start()
    runs = width // side
    for j in range(runs):
        piece = x_ref[:, j * owned : (j + 1) * owned]
        x_wide[j] = piece.astype(F32).reshape(blocks * owned, side)
    taps_copy.wait()
    first_tokens(x_ref, taps_ref, x_wide, ext, owned)
    cos, sin = twist_ref[0], twist_ref[1]

    def some(base):
        first, ahead = first_ref[...], ahead_ref[...]
        back, last = back_ref[...], last_ref[...]
        turned, mixed, columns = {}, {}, {}

        def enter(p):
            held = []
            for c in (2 * p, 2 * p + 1):
                rows = [x_wide[j, pl.ds(base + c, blocks, stride=owned), :] for j in range(runs)]
                held.append(jnp.concatenate(rows, axis=0).astype(BF16))
            turned[p] = enter_pair(jnp.concatenate(held, axis=1), first, cos, sin)

        def multiply(p):
            piece, inside = divmod(base + 2 * p, PIECE)
            if inside == 0:
                fetched(piece).wait()
                if (piece + 1) * PIECE < owned:
                    fetched(piece + 1).start()
            mixed[p] = []
            for i in range(2):
                rows = dot(turned[p][i], ahead)
                re, im = rows[:, :side], rows[:, side:]
                both = filt_ref[base + 2 * p + i]
                fre, fim = both[:, :side], both[:, side:]
                head, rest = split(
                    jnp.concatenate([re * fre - im * fim, re * fim + im * fre], axis=1)
                )
                mixed[p].append(jnp.concatenate([head, rest, head], axis=1))

        def undo(p):
            both = []
            for i in range(2):
                rows = dot(mixed[p][i], back)
                re, im = rows[:, :side], rows[:, side:]
                head, rest = split(
                    jnp.concatenate([re * cos + im * sin, im * cos - re * sin], axis=0)
                )
                both.append(jnp.concatenate([head, rest, head], axis=0))
            columns[p] = jnp.concatenate(both, axis=1)

        def leave(p):
            result = dot(last, columns[p])
            for i in range(2):
                for j in range(runs):
                    y_wide[j, pl.ds(base + 2 * p + i, blocks, stride=owned), :] = result[
                        j * blocks : (j + 1) * blocks, i * side : (i + 1) * side
                    ]

        stages = (enter, multiply, undo, leave)
        pairs = GROUP // 2
        for t in range(pairs + len(stages) - 1):
            for late in (0, 2, 1, 3):
                if 0 <= t - late < pairs:
                    stages[late](t - late)

    part = owned // sems.shape[0]
    copies = []
    for h in range(sems.shape[0]):
        for step in range(part // GROUP):
            some(h * part + step * GROUP)

        size = blocks // sems.shape[1]
        for p in range(sems.shape[1]):
            cut = pl.ds(p * size, size)
            for j in range(runs):
                rows = y_wide[j, p * size * owned : (p + 1) * size * owned]
                rows = rows.reshape(size, owned, side)[:, h * part : (h + 1) * part]
                done[h, cut, :, j * side : (j + 1) * side] = rows.astype(BF16)
            copies.append(
                pltpu.make_async_copy(
                    done.at[h, cut], out_ref.at[cut, pl.ds(h * part, part)], sems.at[h, p]
                )
            )
            copies[-1].start()
    for copy in copies:
        copy.wait()


def product_kernel(q_ref, long_ref, out_ref, done, sems):
    chunks = sems.shape[0]
    rows = done.shape[0] // chunks
    copies = []
    for i in range(chunks):
        cut = pl.ds(i * rows, rows)
        done[cut] = (q_ref[cut].astype(F32) * long_ref[cut].astype(F32)).astype(BF16)
        copies.append(pltpu.make_async_copy(done.at[cut], out_ref.at[cut], sems.at[i]))
        copies[-1].start()
    for copy in copies:
        copy.wait()


def cost(flops, size):
    return pl.CostEstimate(flops=flops, bytes_accessed=size, transcendentals=0)


def params(limit=VMEM_LIMIT):
    return pltpu.CompilerParams(vmem_limit_bytes=limit)


def local(queries, keys, values, short_taps, long_filter, skip_gain):
    ctx_count = lax.axis_size("ctx")
    width, tokens = queries.shape
    owned = width // ctx_count
    side = 128
    runs = tokens // side
    first_plain, first_held, twist, ahead, back, last = (
        jnp.asarray(t) for t in transform_tables(side, runs)
    )

    far = pl.BlockSpec(memory_space=pltpu.HBM)
    whole = pl.BlockSpec(memory_space=pltpu.VMEM)
    shift = [(i, i + 1) for i in range(ctx_count - 1)]

    shape = jax.ShapeDtypeStruct((width, tokens), BF16)
    chunks = 8
    held_rows = runs * owned + RIM
    with jax.named_scope("gate"):
        gated = pl.pallas_call(
            gate_kernel,
            in_specs=[far, far, far],
            out_specs=far,
            out_shape=jax.ShapeDtypeStruct((ctx_count, held_rows, side), BF16),
            scratch_shapes=[
                pltpu.VMEM((4, 2, RIM + tokens, 128), F32),
                pltpu.VMEM((2, width, tokens), BF16),
                pltpu.VMEM((ctx_count, held_rows, side), BF16),
                pltpu.VMEM(short_taps.shape, F32),
                pltpu.SemaphoreType.DMA((2, chunks)),
                pltpu.SemaphoreType.DMA((chunks,)),
                pltpu.SemaphoreType.DMA,
            ],
            compiler_params=params(VMEM_MOST),
            cost_estimate=cost(30 * width * tokens, 6 * width * tokens),
        )(keys, values, short_taps)
    arrived = lax.all_to_all(gated, "ctx", split_axis=0, concat_axis=0, tiled=True)
    own_taps = lax.dynamic_slice_in_dim(short_taps, lax.axis_index("ctx") * owned, owned, 2)
    own_taps = jnp.pad(own_taps[1:], ((0, 0), (0, RIM - TAPS), (0, 0))).reshape(2 * RIM, owned)
    own_taps = jnp.tile(own_taps, (1, side // owned))
    later_queries, _ = lax.optimization_barrier((queries, gated))
    with jax.named_scope("query_tail"):
        query_tail = pl.pallas_call(
            tail_kernel,
            in_specs=[far],
            out_specs=whole,
            out_shape=jax.ShapeDtypeStruct((2 * RIM, width), BF16),
            scratch_shapes=[pltpu.VMEM((width, 128), BF16), pltpu.SemaphoreType.DMA((4,))],
            compiler_params=params(),
            cost_estimate=cost(width * 128, 2 * width * 128),
        )(later_queries)
    query_halo = lax.ppermute(query_tail, "ctx", shift)
    with jax.named_scope("filter"):
        spectrum = pl.pallas_call(
            filter_kernel,
            in_specs=[whole, pl.BlockSpec(memory_space=pltpu.SMEM), whole, whole, whole],
            out_specs=far,
            out_shape=jax.ShapeDtypeStruct((owned, side, 2 * side), F32),
            scratch_shapes=[
                pltpu.VMEM((owned, side, 2 * side), F32),
                pltpu.SemaphoreType.DMA((owned // PIECE,)),
            ],
            compiler_params=params(VMEM_FILTER),
            cost_estimate=cost(owned * side**3 * 16, 5 << 20),
        )(long_filter.reshape(owned, side, side), skip_gain, first_plain, twist, ahead)
    spectrum, query_halo = lax.optimization_barrier((spectrum, query_halo))
    with jax.named_scope("query"):
        q_short = pl.pallas_call(
            query_kernel,
            in_specs=[whole] * 3,
            out_specs=whole,
            out_shape=shape,
            scratch_shapes=[pltpu.VMEM((RIM + tokens, 128), F32)],
            compiler_params=params(),
            cost_estimate=cost(15 * width * tokens, 4 * width * tokens),
        )(later_queries, query_halo, short_taps)
    wide = pltpu.VMEM((runs, ctx_count * owned, side), F32)
    parts = 2
    with jax.named_scope("long"):
        long = pl.pallas_call(
            long_kernel,
            in_specs=[whole, far, far] + [whole] * 5,
            out_specs=far,
            out_shape=jax.ShapeDtypeStruct((ctx_count, owned, tokens), BF16),
            scratch_shapes=[
                wide,
                wide,
                pltpu.VMEM((owned, side, 2 * side), F32),
                pltpu.VMEM((2 * RIM, side), F32),
                pltpu.VMEM((2, ctx_count * owned // side, 2 * RIM, side), F32),
                pltpu.VMEM((parts, ctx_count, owned // parts, tokens), BF16),
                pltpu.SemaphoreType.DMA((parts, 4)),
                pltpu.SemaphoreType.DMA((owned // PIECE,)),
                pltpu.SemaphoreType.DMA,
            ],
            compiler_params=params(VMEM_SOME),
            cost_estimate=cost(owned * side**3 * 32, 7 << 20),
        )(arrived, spectrum, own_taps, first_held, twist, ahead, back, last)
    returned = lax.all_to_all(long, "ctx", split_axis=0, concat_axis=0, tiled=True)
    returned = returned.reshape(width, tokens)
    with jax.named_scope("product"):
        return pl.pallas_call(
            product_kernel,
            in_specs=[whole, whole],
            out_specs=far,
            out_shape=shape,
            scratch_shapes=[pltpu.VMEM((width, tokens), BF16), pltpu.SemaphoreType.DMA((8,))],
            compiler_params=params(),
            cost_estimate=cost(width * tokens, 6 * width * tokens),
        )(q_short, returned)


def solution(mesh):
    placed = (
        P("ch", "ctx"),
        P("ch", "ctx"),
        P("ch", "ctx"),
        P(None, None, "ch"),
        P("ch", "ctx", None),
        P("ch", "ctx"),
    )
    return jax.shard_map(
        local, mesh=mesh, in_specs=placed, out_specs=P("ch", "ctx"), check_vma=False
    )
```

```python
import jax
import jax.numpy as jnp
import numpy as np
from jax import lax
from jax.experimental import pallas as pl
from jax.experimental.pallas import tpu as pltpu
from jax.sharding import PartitionSpec as P

VMEM_LIMIT = 24 * 1024 * 1024
VMEM_FILTER = 60 * 1024 * 1024
VMEM_SOME = 52 * 1024 * 1024
VMEM_MOST = 63 * 1024 * 1024
RIM = 8
TAPS = 7
GROUP = 16
PIECE = 4
BF16, F32 = jnp.bfloat16, jnp.float32


def head_and_rest(table):
    head = table.astype(np.float32).astype(jnp.bfloat16)
    rest = (table - head.astype(np.float64)).astype(np.float32).astype(jnp.bfloat16)
    return head, rest


def transform_tables(side, runs):
    length = side * side
    k = np.arange(side)
    natural = np.arange(side)
    blocks = side // runs
    held = (np.arange(blocks)[None, :] * runs + np.arange(runs)[:, None]).reshape(-1)

    def first(order):
        angle = 2 * np.pi * (k[:, None] + 0.25) * order[None, :] / side
        both = np.concatenate([np.cos(angle), np.sin(angle)], axis=0)
        return np.concatenate(head_and_rest(both), axis=1)

    turn = 2 * np.pi * (k[:, None] + 0.25) * natural[None, :] / length
    twist = np.stack([np.cos(turn), np.sin(turn)]).astype(np.float32)
    angle = 2 * np.pi * (natural[:, None] * k[None, :] % side) / side
    cos, sin = np.cos(angle), np.sin(angle)

    def second(matrix):
        head, rest = head_and_rest(matrix)
        return np.concatenate([head, head, rest], axis=0)

    ahead = second(np.block([[cos, sin], [-sin, cos]]))
    back = second(np.block([[cos, -sin], [sin, cos]]))
    angle = 2 * np.pi * held[:, None] * (k[None, :] + 0.25) / side
    head, rest = head_and_rest(np.concatenate([np.cos(angle), np.sin(angle)], axis=1) / length)
    last = np.concatenate([head, head, rest], axis=1)
    return first(natural), first(held), twist, ahead, back, last


def split(array):
    head = array.astype(BF16)
    return head, (array - head.astype(F32)).astype(BF16)


def dot(a, b):
    return jnp.dot(a, b, preferred_element_type=F32)


def fetch(source, target, sems, columns):
    rows = target.shape[0] // sems.shape[0]
    copies = []
    for i in range(sems.shape[0]):
        cut = pl.ds(i * rows, rows)
        copies.append(
            pltpu.make_async_copy(source.at[cut, columns], target.at[cut], sems.at[i])
        )
        copies[-1].start()
    return copies


def tail_kernel(q_ref, out_ref, held, sems):
    copies = fetch(q_ref, held, sems, pl.ds(q_ref.shape[1] - 128, 128))
    rows = held.shape[0] // len(copies)
    for i, copy in enumerate(copies):
        copy.wait()
        out_ref[:, i * rows : (i + 1) * rows] = held[i * rows : (i + 1) * rows].T[-2 * RIM :]


def short_conv(block, halo, taps_ref, which, c0, ext):
    count = block.shape[0]
    ext[:RIM] = halo
    ext[RIM:] = block
    channels = pl.ds(c0, 128)
    total = taps_ref[which, 0:1, channels] * block
    for j in range(1, taps_ref.shape[1]):
        total = total + taps_ref[which, j : j + 1, channels] * ext[RIM - j : RIM - j + count]
    return total


def gate_kernel(
    k_ref, v_ref, far_ref, out_ref, ext, held, done, taps_ref, sems_in, sems_out, sem_taps
):
    width, tokens = k_ref.shape
    runs = tokens // 128
    owned = width // out_ref.shape[0]
    fit = 128 // owned
    chunks = sems_out.shape[0]
    rows = width // chunks
    lane = lax.broadcasted_iota(jnp.int32, (RIM, 128), 1) // owned
    nothing = jnp.zeros((RIM, 128), F32)
    turn = lax.axis_index("ctx") % fit

    def fetch(i):
        cut = pl.ds(i * rows, rows)
        for n, ref in enumerate((k_ref, v_ref)):
            yield pltpu.make_async_copy(ref.at[cut], held.at[n, cut], sems_in.at[n, i])

    def send(i):
        cut = pl.ds(i * rows // owned, rows // owned)
        return pltpu.make_async_copy(done.at[cut], out_ref.at[cut], sems_out.at[i])

    taps_copy = pltpu.make_async_copy(far_ref, taps_ref, sem_taps)
    taps_copy.start()
    for i in range(chunks):
        for copy in fetch(i):
            copy.start()
    taps_copy.wait()
    for i in range(chunks):
        for copy in fetch(i):
            copy.wait()
        for c in range(i * rows, (i + 1) * rows, 128):
            both, rims = [], []
            for n in range(2):
                turned = held[n, c : c + 128].T.astype(F32)
                rows_ext = ext.at[c // 128 % ext.shape[0], n]
                both.append(short_conv(turned, nothing, taps_ref, n + 1, c, rows_ext))
                rims.append((turned[tokens - RIM :], turned[:RIM]))
            gated = (both[0] * both[1]).astype(BF16)
            first = c // owned
            for j in range(runs):
                piece = gated[j * 128 : (j + 1) * 128].T
                done[first : first + fit, j * owned : (j + 1) * owned] = piece.reshape(fit, owned, 128)
            sides = (rims[0][1], rims[0][0], rims[1][1], rims[1][0])
            for d in range(fit):
                rim = nothing
                for g, side in enumerate(sides):
                    moved = pltpu.roll(side, (g - d) % fit * owned, 1)
                    rim = jnp.where(lane == g, moved, rim)
                rim = pltpu.roll(rim, turn * owned, 1)
                done[first + d, runs * owned :] = rim.astype(BF16)
        send(i).start()
    for i in range(chunks):
        send(i).wait()


def query_kernel(q_ref, halo_ref, taps_ref, out_ref, ext):
    width = q_ref.shape[0]
    for c in range(0, width, 128):
        halo = halo_ref[:, c : c + 128].astype(F32)
        turned = q_ref[c : c + 128].T.astype(F32)
        queries = short_conv(turned, halo[RIM:], taps_ref, 0, c, ext)
        out_ref[c : c + 128] = queries.astype(BF16).T


def enter_pair(pair, first, cos, sin):
    side = pair.shape[0]
    both = dot(first, jnp.concatenate([pair, pair], axis=0))
    parts = []
    for i in range(2):
        re = both[:side, i * side : (i + 1) * side]
        im = both[side:, i * side : (i + 1) * side]
        turned = jnp.concatenate([re * cos - im * sin, re * sin + im * cos], axis=1)
        head, rest = split(turned)
        parts.append(jnp.concatenate([head, rest, head], axis=1))
    return parts


def to_spectrum(pairs, first, twist, ahead):
    return [
        dot(part, ahead) for pair in pairs for part in enter_pair(pair, first, twist[0], twist[1])
    ]


def filter_kernel(
    filt_ref, gain_ref, first_ref, twist_ref, ahead_ref, out_ref, done, sems
):
    owned, side, _ = filt_ref.shape

    def send(step):
        cut = pl.ds(step * PIECE, PIECE)
        return pltpu.make_async_copy(done.at[cut], out_ref.at[cut], sems.at[step])

    @pl.loop(0, owned // PIECE)
    def _(step):
        base = step * PIECE
        pairs = [
            jnp.concatenate([filt_ref[base + c], filt_ref[base + c + 1]], axis=1)
            for c in range(0, PIECE, 2)
        ]
        spectrum = to_spectrum(pairs, first_ref[...], twist_ref, ahead_ref[...])
        for c, rows in enumerate(spectrum):
            re, im = rows[:, :side] + gain_ref[0, base + c], rows[:, side:]
            done[base + c] = jnp.concatenate([re, im], axis=1)
        send(step).start()

    for step in range(owned // PIECE):
        send(step).wait()


def first_tokens(x_ref, taps_ref, x_wide, ext, owned):
    blocks, rows, lanes = x_ref.shape
    fit = lanes // owned
    steps = blocks // fit
    rims = x_ref[:, rows - RIM :].astype(F32)
    before = jnp.concatenate([jnp.zeros((1, RIM, lanes), F32), rims[:-1]], axis=0)
    group = lax.broadcasted_iota(jnp.int32, (RIM, lanes), 1) // owned
    for q in range(steps):
        for n in range(2):
            for start, source in ((0, before), (RIM, rims)):
                packed = source[q * fit]
                for i in range(1, fit):
                    packed = jnp.where(group == (i + 2 * n) % fit, source[q * fit + i], packed)
                ext[n, q, start : start + RIM] = packed
    sums = []
    for n in range(2):
        total = taps_ref[RIM * n : RIM * n + 1] * ext[n, :, RIM:]
        for j in range(1, TAPS):
            tap = taps_ref[RIM * n + j : RIM * n + j + 1]
            total = total + tap * ext[n, :, RIM - j : 2 * RIM - j]
        sums.append(total)
    for q in range(steps):
        gated = sums[0][q] * pltpu.roll(sums[1][q], 2 * owned, 1)
        x_wide[0, q * lanes : (q + 1) * lanes, :RIM] = gated.T.astype(BF16).astype(F32)


def long_kernel(
    x_ref, far_ref, far_taps_ref, first_ref, twist_ref, ahead_ref, back_ref, last_ref, out_ref,
    x_wide, y_wide, filt_ref, taps_ref, ext, done, sems, sems_in, sem_taps,
):
    blocks, owned, width = out_ref.shape
    side = filt_ref.shape[1]

    def fetched(piece):
        cut = pl.ds(piece * PIECE, PIECE)
        return pltpu.make_async_copy(far_ref.at[cut], filt_ref.at[cut], sems_in.at[piece])

    taps_copy = pltpu.make_async_copy(far_taps_ref, taps_ref, sem_taps)
    taps_copy.start()
    fetched(0).start()
    runs = width // side
    for j in range(runs):
        piece = x_ref[:, j * owned : (j + 1) * owned]
        x_wide[j] = piece.astype(F32).reshape(blocks * owned, side)
    taps_copy.wait()
    first_tokens(x_ref, taps_ref, x_wide, ext, owned)
    cos, sin = twist_ref[0], twist_ref[1]

    def some(base):
        first, ahead = first_ref[...], ahead_ref[...]
        back, last = back_ref[...], last_ref[...]
        turned, mixed, columns = {}, {}, {}

        def enter(p):
            held = []
            for c in (2 * p, 2 * p + 1):
                rows = [x_wide[j, pl.ds(base + c, blocks, stride=owned), :] for j in range(runs)]
                held.append(jnp.concatenate(rows, axis=0).astype(BF16))
            turned[p] = enter_pair(jnp.concatenate(held, axis=1), first, cos, sin)

        def multiply(p):
            piece, inside = divmod(base + 2 * p, PIECE)
            if inside == 0:
                fetched(piece).wait()
                if (piece + 1) * PIECE < owned:
                    fetched(piece + 1).start()
            mixed[p] = []
            for i in range(2):
                rows = dot(turned[p][i], ahead)
                re, im = rows[:, :side], rows[:, side:]
                both = filt_ref[base + 2 * p + i]
                fre, fim = both[:, :side], both[:, side:]
                head, rest = split(
                    jnp.concatenate([re * fre - im * fim, re * fim + im * fre], axis=1)
                )
                mixed[p].append(jnp.concatenate([head, rest, head], axis=1))

        def undo(p):
            both = []
            for i in range(2):
                rows = dot(mixed[p][i], back)
                re, im = rows[:, :side], rows[:, side:]
                head, rest = split(
                    jnp.concatenate([re * cos + im * sin, im * cos - re * sin], axis=0)
                )
                both.append(jnp.concatenate([head, rest, head], axis=0))
            columns[p] = jnp.concatenate(both, axis=1)

        def leave(p):
            result = dot(last, columns[p])
            for i in range(2):
                for j in range(runs):
                    y_wide[j, pl.ds(base + 2 * p + i, blocks, stride=owned), :] = result[
                        j * blocks : (j + 1) * blocks, i * side : (i + 1) * side
                    ]

        stages = (enter, multiply, undo, leave)
        pairs = GROUP // 2
        for t in range(pairs + len(stages) - 1):
            for late in (0, 2, 1, 3):
                if 0 <= t - late < pairs:
                    stages[late](t - late)

    part = owned // sems.shape[0]
    copies = []
    for h in range(sems.shape[0]):
        for step in range(part // GROUP):
            some(h * part + step * GROUP)

        size = blocks // sems.shape[1]
        for p in range(sems.shape[1]):
            cut = pl.ds(p * size, size)
            for j in range(runs):
                rows = y_wide[j, p * size * owned : (p + 1) * size * owned]
                rows = rows.reshape(size, owned, side)[:, h * part : (h + 1) * part]
                done[h, cut, :, j * side : (j + 1) * side] = rows.astype(BF16)
            copies.append(
                pltpu.make_async_copy(
                    done.at[h, cut], out_ref.at[cut, pl.ds(h * part, part)], sems.at[h, p]
                )
            )
            copies[-1].start()
    for copy in copies:
        copy.wait()


def product_kernel(q_ref, long_ref, out_ref, done, sems):
    chunks = sems.shape[0]
    rows = done.shape[0] // chunks
    copies = []
    for i in range(chunks):
        cut = pl.ds(i * rows, rows)
        done[cut] = (q_ref[cut].astype(F32) * long_ref[cut].astype(F32)).astype(BF16)
        copies.append(pltpu.make_async_copy(done.at[cut], out_ref.at[cut], sems.at[i]))
        copies[-1].start()
    for copy in copies:
        copy.wait()


def cost(flops, size):
    return pl.CostEstimate(flops=flops, bytes_accessed=size, transcendentals=0)


def params(limit=VMEM_LIMIT):
    return pltpu.CompilerParams(vmem_limit_bytes=limit)


def local(queries, keys, values, short_taps, long_filter, skip_gain):
    ctx_count = lax.axis_size("ctx")
    width, tokens = queries.shape
    owned = width // ctx_count
    side = 128
    runs = tokens // side
    first_plain, first_held, twist, ahead, back, last = (
        jnp.asarray(t) for t in transform_tables(side, runs)
    )

    far = pl.BlockSpec(memory_space=pltpu.HBM)
    whole = pl.BlockSpec(memory_space=pltpu.VMEM)
    shift = [(i, i + 1) for i in range(ctx_count - 1)]

    shape = jax.ShapeDtypeStruct((width, tokens), BF16)
    chunks = 8
    held_rows = runs * owned + RIM
    with jax.named_scope("gate"):
        gated = pl.pallas_call(
            gate_kernel,
            in_specs=[far, far, far],
            out_specs=far,
            out_shape=jax.ShapeDtypeStruct((ctx_count, held_rows, side), BF16),
            scratch_shapes=[
                pltpu.VMEM((4, 2, RIM + tokens, 128), F32),
                pltpu.VMEM((2, width, tokens), BF16),
                pltpu.VMEM((ctx_count, held_rows, side), BF16),
                pltpu.VMEM(short_taps.shape, F32),
                pltpu.SemaphoreType.DMA((2, chunks)),
                pltpu.SemaphoreType.DMA((chunks,)),
                pltpu.SemaphoreType.DMA,
            ],
            compiler_params=params(VMEM_MOST),
            cost_estimate=cost(30 * width * tokens, 6 * width * tokens),
        )(keys, values, short_taps)
    arrived = lax.all_to_all(gated, "ctx", split_axis=0, concat_axis=0, tiled=True)
    own_taps = lax.dynamic_slice_in_dim(short_taps, lax.axis_index("ctx") * owned, owned, 2)
    own_taps = jnp.pad(own_taps[1:], ((0, 0), (0, RIM - TAPS), (0, 0))).reshape(2 * RIM, owned)
    own_taps = jnp.tile(own_taps, (1, side // owned))
    later_queries, _ = lax.optimization_barrier((queries, gated))
    with jax.named_scope("query_tail"):
        query_tail = pl.pallas_call(
            tail_kernel,
            in_specs=[far],
            out_specs=whole,
            out_shape=jax.ShapeDtypeStruct((2 * RIM, width), BF16),
            scratch_shapes=[pltpu.VMEM((width, 128), BF16), pltpu.SemaphoreType.DMA((4,))],
            compiler_params=params(),
            cost_estimate=cost(width * 128, 2 * width * 128),
        )(later_queries)
    query_halo = lax.ppermute(query_tail, "ctx", shift)
    with jax.named_scope("filter"):
        spectrum = pl.pallas_call(
            filter_kernel,
            in_specs=[whole, pl.BlockSpec(memory_space=pltpu.SMEM), whole, whole, whole],
            out_specs=far,
            out_shape=jax.ShapeDtypeStruct((owned, side, 2 * side), F32),
            scratch_shapes=[
                pltpu.VMEM((owned, side, 2 * side), F32),
                pltpu.SemaphoreType.DMA((owned // PIECE,)),
            ],
            compiler_params=params(VMEM_FILTER),
            cost_estimate=cost(owned * side**3 * 16, 5 << 20),
        )(long_filter.reshape(owned, side, side), skip_gain, first_plain, twist, ahead)
    spectrum, query_halo = lax.optimization_barrier((spectrum, query_halo))
    with jax.named_scope("query"):
        q_short = pl.pallas_call(
            query_kernel,
            in_specs=[whole] * 3,
            out_specs=whole,
            out_shape=shape,
            scratch_shapes=[pltpu.VMEM((RIM + tokens, 128), F32)],
            compiler_params=params(),
            cost_estimate=cost(15 * width * tokens, 4 * width * tokens),
        )(later_queries, query_halo, short_taps)
    wide = pltpu.VMEM((runs, ctx_count * owned, side), F32)
    parts = 2
    with jax.named_scope("long"):
        long = pl.pallas_call(
            long_kernel,
            in_specs=[whole, far, far] + [whole] * 5,
            out_specs=far,
            out_shape=jax.ShapeDtypeStruct((ctx_count, owned, tokens), BF16),
            scratch_shapes=[
                wide,
                wide,
                pltpu.VMEM((owned, side, 2 * side), F32),
                pltpu.VMEM((2 * RIM, side), F32),
                pltpu.VMEM((2, ctx_count * owned // side, 2 * RIM, side), F32),
                pltpu.VMEM((parts, ctx_count, owned // parts, tokens), BF16),
                pltpu.SemaphoreType.DMA((parts, 4)),
                pltpu.SemaphoreType.DMA((owned // PIECE,)),
                pltpu.SemaphoreType.DMA,
            ],
            compiler_params=params(VMEM_SOME),
            cost_estimate=cost(owned * side**3 * 32, 7 << 20),
        )(arrived, spectrum, own_taps, first_held, twist, ahead, back, last)
    returned = lax.all_to_all(long, "ctx", split_axis=0, concat_axis=0, tiled=True)
    returned = returned.reshape(width, tokens)
    with jax.named_scope("product"):
        return pl.pallas_call(
            product_kernel,
            in_specs=[whole, whole],
            out_specs=far,
            out_shape=shape,
            scratch_shapes=[pltpu.VMEM((width, tokens), BF16), pltpu.SemaphoreType.DMA((8,))],
            compiler_params=params(),
            cost_estimate=cost(width * tokens, 6 * width * tokens),
        )(q_short, returned)


def solution(mesh):
    placed = (
        P("ch", "ctx"),
        P("ch", "ctx"),
        P("ch", "ctx"),
        P(None, None, "ch"),
        P("ch", "ctx", None),
        P("ch", "ctx"),
    )
    return jax.shard_map(
        local, mesh=mesh, in_specs=placed, out_specs=P("ch", "ctx"), check_vma=False
    )
```
